512 devices in a mesh: dp: 16 (over y, z_lo), fsdp: 32 (over x, z_hi, core).
Axes of the slice: x: 4, y: 4, z: 16 (z_hi: 4, z_lo: 4; z = z_hi * 4 + z_lo), core: 2. Of those that a mesh axis runs over, the one named last changes fastest.
Arguments:
- hidden: bfloat16 [8192, 16384], P('dp', 'fsdp'), may hold values from -200 to 200
- upstream: bfloat16 [8192, 4096], P('dp', 'fsdp'), may hold values from -16 to 16
- down_weight: bfloat16 [16384, 4096], P('fsdp', 'dp'), may hold values from -0.09375 to 0.09375
- mask_logits: float32 [4096, 6, 4096], P('fsdp', None, 'dp'), may hold values from -10 to 610
- gumbel_noise: float32 [4096, 6, 4096], P('fsdp', None, 'dp'), may hold values from -3 to 14
Outputs:
- grad_hidden: bfloat16 [8192, 16384], P('dp', 'fsdp')
- logit_step: float32 [4096, 6, 4096], P('fsdp', None, 'dp')
The draws below stay inside these ranges and needn't reach their ends.
All inputs are finite; a program needn't handle non-finite values.
Results may differ from the reference program's by a relative error of at most 0.02.
Values may be sent and summed in bfloat16 or wider, within the bound.
No kernel may reach another device: no remote copies, remote signals or barrier semaphores. Data moves between devices by JAX's collectives and lax.ppermute only.
A program may use at most 128 MiB of HBM per device.

```python
import jax
import jax.numpy as jnp
import numpy as np
from jax import lax

D = 4096
FF = 16384
TOK_DEV = 512
TOKENS = 8192
GROUPS = 4096
N_DP = 16


def token_signal(key):
    key_sign = jax.random.fold_in(key, 5)
    position = jnp.arange(TOKENS, dtype=jnp.float32)[:, None] / TOKENS
    sign_draw = jax.random.truncated_normal(key_sign, -3.0, 3.0, (TOKENS, 1), jnp.float32)
    return sign_draw * jnp.sqrt(0.3 + 1.7 * position) * (1.2 * TOKENS ** (-0.25))


def draw_hidden(key, part):
    shared = token_signal(key)
    key = jax.random.fold_in(key, 11)
    key_base = jax.random.fold_in(key, 0)
    key_rows = jax.random.fold_in(key, 1)
    key_cols = jax.random.fold_in(key, 2)
    key_pattern = jax.random.fold_in(key, 4)
    row_scale = jnp.exp(jax.random.uniform(key_rows, (TOKENS, 1), jnp.float32, 0.0, 2.302585))
    col_scale = jnp.exp(jax.random.uniform(key_cols, (1, FF), jnp.float32, 0.0, 2.302585))
    ramp = 0.6 + 1.2 * jnp.arange(FF, dtype=jnp.float32)[None, :] / FF
    pattern = jax.random.truncated_normal(key_pattern, -3.0, 3.0, (1, FF), jnp.float32)
    base = jax.random.truncated_normal(key_base, -6.0, 6.0, (TOKENS, FF), jnp.float32)
    base = base + shared * pattern
    return jnp.clip(base * row_scale * col_scale * ramp / 6.0, -199.0, 199.0).astype(jnp.bfloat16)


def draw_upstream(key, part):
    shared = token_signal(key)
    key = jax.random.fold_in(key, 53)
    key_base, key_pattern = jax.random.split(key, 2)
    position = jnp.arange(D, dtype=jnp.float32)[None, :] / D
    pattern = jax.random.truncated_normal(key_pattern, -3.0, 3.0, (1, D), jnp.float32)
    base = jax.random.truncated_normal(key_base, -6.0, 6.0, (TOKENS, D), jnp.float32)
    ramp = 0.5 + 2.0 * position
    base = base + shared * pattern
    return jnp.clip(base * ramp, -15.9, 15.9).astype(jnp.bfloat16)


def draw_mask_logits(key, part):
    key = jax.random.fold_in(key, 37)
    key_base = jax.random.fold_in(key, 0)
    shape = (GROUPS, 6, D)
    return jnp.clip(1.5 * jax.random.normal(key_base, shape, jnp.float32), -10.0, 10.0)


def draw_gumbel_noise(key, part):
    key = jax.random.fold_in(key, 23)
    uniform_draw = jax.random.uniform(key, (GROUPS, 6, D), jnp.float32, 1e-06, 1.0 - 1e-06)
    return -jnp.log(-jnp.log(uniform_draw))


def block_levels(rng, extent, shards, low, high):
    gain = 1.0
    for dim, shards_of in shards:
        steps = jax.random.uniform(jax.random.fold_in(jax.random.fold_in(rng, 6), dim), (shards_of,), jnp.float32, low / len(shards), high / len(shards))
        gain = gain * jnp.repeat(jnp.exp(steps), extent[dim] // shards_of).reshape((-1,) + (1,) * (len(extent) - 1 - dim))
    return gain


def normal_values(own_key, dims, width, most, pieces=(), kind=jnp.bfloat16):
    drawn = width * jax.random.normal(own_key, dims, jnp.float32)
    if pieces:
        drawn = drawn * block_levels(own_key, dims, pieces, -0.22, 0.18)
    return jnp.clip(drawn, -most, most).astype(kind)


def setup_inputs(seed: int = 0) -> dict:
    keys = jax.random.split(jax.random.key(seed), 6)
    return {
        "hidden": draw_hidden(jax.random.fold_in(keys[5], 71), 0),
        "upstream": draw_upstream(jax.random.fold_in(keys[5], 71), 0),
        "down_weight": normal_values(keys[2], (FF, D), D ** -0.5, 0.09375, ((0, 32), (1, 16))),
        "mask_logits": draw_mask_logits(jax.random.fold_in(keys[5], 71), 0),
        "gumbel_noise": draw_gumbel_noise(jax.random.fold_in(keys[5], 71), 0),
    }


CANDIDATES = np.array([[1, 1, 0, 0], [1, 0, 1, 0], [1, 0, 0, 1], [0, 1, 1, 0], [0, 1, 0, 1], [0, 0, 1, 1]], np.float32)
TEMPER = 2.0

def soft_probs(mask_logits, gumbel_noise):
    return jax.nn.softmax((mask_logits + gumbel_noise) / TEMPER, axis=1)

def build_masked(weight_groups, rounded):
    table = jnp.asarray(CANDIDATES, jnp.float32)
    keep = jnp.einsum('gkc,kj->gjc', rounded.astype(jnp.float32), table)
    return (weight_groups.astype(jnp.float32) * keep).astype(jnp.bfloat16)

def reference(hidden, upstream, down_weight, mask_logits, gumbel_noise):
    probs = soft_probs(mask_logits, gumbel_noise)
    rounded = probs.astype(jnp.bfloat16)
    masked = build_masked(down_weight.reshape(GROUPS, 4, D), rounded).reshape(FF, D)
    grad_hidden = jnp.dot(upstream, masked.T, preferred_element_type=jnp.float32).astype(jnp.bfloat16)

    def add_block(carried, block_index):
        start_row = (block_index * TOK_DEV).astype(jnp.int32)
        block_hidden = lax.dynamic_slice_in_dim(hidden, start_row, TOK_DEV, 0)
        block_upstream = lax.dynamic_slice_in_dim(upstream, start_row, TOK_DEV, 0)
        partial_sum = jnp.dot(block_hidden.T, block_upstream, preferred_element_type=jnp.float32)
        partial_sum = lax.optimization_barrier(partial_sum.astype(jnp.bfloat16)).astype(jnp.float32)
        return (carried + partial_sum, None)
    grad_masked, _ = lax.scan(add_block, jnp.zeros((FF, D), jnp.float32), jnp.arange(N_DP, dtype=jnp.int32))
    table = jnp.asarray(CANDIDATES, jnp.float32)
    product = (grad_masked * down_weight.astype(jnp.float32)).reshape(GROUPS, 4, D)
    grad_probs = jnp.einsum('gjc,kj->gkc', product, table)
    grad_logits = probs * (grad_probs - lax.optimization_barrier(jnp.sum(probs * grad_probs, axis=1, keepdims=True))) / TEMPER
    mean_square = jnp.mean(grad_logits * grad_logits)
    logit_step = grad_logits / jnp.sqrt(mean_square + 1e-06)
    return (grad_hidden, logit_step)
```

```python
import jax
import jax.numpy as jnp
import numpy as np
from jax import lax
from jax.experimental import pallas as pl
from jax.experimental.pallas import tpu as pltpu
from jax.sharding import Mesh, PartitionSpec as P

PAIRS = ((0, 1), (0, 2), (0, 3), (1, 2), (1, 3), (2, 3))
TEMPER = 2.0
VMEM = 48 * 1024 * 1024


def grad_masked_kernel(place, hid, a0, a1, a2, a3, b0, b1, b2, b3, o0, o1, o2, o3):
    l, x, c = place[0], place[1], place[2]
    own, other = (a0, a1, a2, a3), (b0, b1, b2, b3)
    for e, out in enumerate((o0, o1, o2, o3)):
        col = lax.rem(l + e, 4)
        total = None
        for k in range(4):
            tok = lax.rem(x + 4 - k, 4)
            mine, theirs = own[k][col], other[k][col]
            first = jnp.where(c == 0, mine, theirs)
            second = jnp.where(c == 0, theirs, mine)
            part = jnp.dot(
                hid[tok], jnp.concatenate([first, second], axis=1), preferred_element_type=jnp.float32
            )
            total = part if total is None else total + part
        out[...] = total.astype(out.dtype)


def grad_hidden_kernel(place, mt, a0, a1, a2, a3, b0, b1, b2, b3, out):
    x, c = place[1], place[2]
    own, other = (a0, a1, a2, a3), (b0, b1, b2, b3)
    for k in range(4):
        tok = lax.rem(x + 4 - k, 4)
        pieces = []
        for col in range(4):
            mine, theirs = own[k][col], other[k][col]
            pieces += [jnp.where(c == 0, mine, theirs), jnp.where(c == 0, theirs, mine)]
        out[tok] = jnp.dot(
            jnp.concatenate(pieces, axis=1), mt[...], preferred_element_type=jnp.float32
        ).astype(out.dtype)


def grad_logits_kernel(g0, g1, g2, g3, w, probs, out, squares):
    prod = []
    for j in range(4):
        rows = pl.ds(128 * j, 128)
        total = (
            g0[rows, :]
            + g1[rows, :].astype(jnp.float32)
            + g2[rows, :].astype(jnp.float32)
            + g3[rows, :].astype(jnp.float32)
        )
        prod.append(total * w[rows, :].astype(jnp.float32))
    grads = [prod[a] + prod[b] for a, b in PAIRS]
    mean = sum(probs[k] * grads[k] for k in range(6))
    sums = jnp.zeros((128, 256), jnp.float32)
    for k in range(6):
        value = probs[k] * (grads[k] - mean) * (1.0 / TEMPER)
        out[k] = value
        sums = sums + value * value
    sums = jnp.sum(sums, axis=0, keepdims=True)
    squares[...] = sums[:, :128] + sums[:, 128:]


def body(hidden, upstream, down_weight, mask_logits, gumbel_noise):
    y, l, x, h, c = (lax.axis_index(a) for a in ("y", "l", "x", "h", "c"))
    place = jnp.stack([l, x, c, y]).astype(jnp.int32)

    up = lax.all_to_all(jnp.broadcast_to(upstream[None], (4, 512, 128)), "h", 0, 0)

    order = np.zeros((512, 512), np.float32)
    for j in range(4):
        for g in range(128):
            order[j * 128 + g, 4 * g + j] = 1.0
    order = jnp.asarray(order, jnp.bfloat16)
    hid_t = lax.dot_general(
        order, hidden, (((1,), (1,)), ((), ())), preferred_element_type=jnp.float32
    ).astype(jnp.bfloat16)
    hid_all = lax.all_to_all(jnp.broadcast_to(hid_t[None], (4, 512, 512)), "y", 0, 0)

    weight = jnp.dot(order, down_weight, preferred_element_type=jnp.float32).astype(jnp.bfloat16)
    logits = jnp.transpose(mask_logits, (1, 0, 2)) + jnp.transpose(gumbel_noise, (1, 0, 2))
    probs = jax.nn.softmax(logits / TEMPER, axis=0)
    rounded = probs.astype(jnp.bfloat16).astype(jnp.float32)
    keep = [sum(rounded[k] for k in range(6) if j in PAIRS[k]) for j in range(4)]
    masked = jnp.concatenate(
        [(weight[128 * j : 128 * j + 128].astype(jnp.float32) * keep[j]).astype(jnp.bfloat16) for j in range(4)]
    )
    masked_t = lax.dot_general(
        masked, order, (((0,), (0,)), ((), ())), preferred_element_type=jnp.float32
    ).astype(jnp.bfloat16)
    mt = lax.all_to_all(jnp.broadcast_to(masked_t[None], (4, 256, 512)), "l", 0, 0).reshape(1024, 512)

    own = [
        lax.ppermute(up, ("y", "x"), [(b * 4 + a, a * 4 + (b + k) % 4) for b in range(4) for a in range(4)])
        for k in range(4)
    ]
    other = [lax.ppermute(u, "c", [(0, 1), (1, 0)]) for u in own]

    smem = pl.BlockSpec(memory_space=pltpu.SMEM)
    vmem = pl.BlockSpec(memory_space=pltpu.VMEM)
    params = pltpu.CompilerParams(vmem_limit_bytes=VMEM)
    g = pl.pallas_call(
        grad_masked_kernel,
        out_shape=[jax.ShapeDtypeStruct((512, 256), jnp.float32)]
        + [jax.ShapeDtypeStruct((512, 256), jnp.bfloat16)] * 3,
        in_specs=[smem] + [vmem] * 9,
        out_specs=[vmem] * 4,
        compiler_params=params,
        cost_estimate=pl.CostEstimate(flops=2 * 512 * 2048 * 1024, bytes_accessed=7 << 20, transcendentals=0),
        name="grad_masked",
    )(place, hid_all, *own, *other)
    got = [lax.ppermute(g[e], "l", [(i, (i + e) % 4) for i in range(4)]) for e in (1, 2, 3)]

    gh = pl.pallas_call(
        grad_hidden_kernel,
        out_shape=jax.ShapeDtypeStruct((4, 512, 512), jnp.bfloat16),
        in_specs=[smem] + [vmem] * 9,
        out_specs=vmem,
        compiler_params=params,
        cost_estimate=pl.CostEstimate(flops=2 * 512 * 2048 * 1024, bytes_accessed=7 << 20, transcendentals=0),
        name="grad_hidden",
    )(place, mt, *own, *other)
    gh = lax.all_to_all(gh, "y", 0, 0)
    grad_hidden = jnp.sum(gh.astype(jnp.float32), axis=0).astype(jnp.bfloat16)

    grad_logits, squares = pl.pallas_call(
        grad_logits_kernel,
        out_shape=[
            jax.ShapeDtypeStruct((6, 128, 256), jnp.float32),
            jax.ShapeDtypeStruct((1, 128), jnp.float32),
        ],
        in_specs=[vmem] * 6,
        out_specs=[vmem] * 2,
        compiler_params=params,
        cost_estimate=pl.CostEstimate(flops=1 << 21, bytes_accessed=3 << 20, transcendentals=0),
        name="grad_logits",
    )(g[0], *got, weight, probs)
    squares = lax.all_to_all(jnp.broadcast_to(squares, (32, 128)), ("x", "y", "c"), 0, 0, tiled=True)
    squares = jnp.sum(squares, axis=0, keepdims=True)
    squares = lax.all_to_all(jnp.broadcast_to(squares, (16, 128)), ("l", "h"), 0, 0, tiled=True)
    scale = lax.rsqrt(jnp.sum(squares) / (4096 * 6 * 4096) + 1e-06)
    logit_step = jnp.transpose(grad_logits * scale, (1, 0, 2))
    return grad_hidden, logit_step


def solution(mesh):
    fine = Mesh(mesh.devices.reshape(4, 4, 4, 4, 2), ("y", "l", "x", "h", "c"))
    dp, fsdp = ("y", "l"), ("x", "h", "c")
    return jax.shard_map(
        body,
        mesh=fine,
        in_specs=(
            P(dp, fsdp),
            P(dp, fsdp),
            P(fsdp, dp),
            P(fsdp, None, dp),
            P(fsdp, None, dp),
        ),
        out_specs=(P(dp, fsdp), P(fsdp, None, dp)),
        check_vma=False,
    )
```

```python
import jax
import jax.numpy as jnp
import numpy as np
from jax import lax
from jax.experimental import pallas as pl
from jax.experimental.pallas import tpu as pltpu
from jax.sharding import Mesh, PartitionSpec as P

PAIRS = ((0, 1), (0, 2), (0, 3), (1, 2), (1, 3), (2, 3))
TEMPER = 2.0
VMEM = 60 * 1024 * 1024


def stack_kernel(r0, r1, r2, r3, out):
    for d, piece in enumerate((r0, r1, r2, r3)):
        out[d] = piece[...]


def grad_masked_kernel(
    place, hid, a0, a1, a2, a3, b0, b1, b2, b3, o0, o1, o2, o3
):
    l, x, c, y, h = (place[i] for i in range(5))
    own, other = (a0, a1, a2, a3), (b0, b1, b2, b3)
    for e, out in enumerate((o0, o1, o2, o3)):
        col = lax.rem(h + 8 - l - e, 4)
        total = None
        for k in range(4):
            tok = lax.rem(x + 4 - k, 4)
            mine, theirs = own[k][col], other[k][col]
            first = jnp.where(c == 0, mine, theirs)
            second = jnp.where(c == 0, theirs, mine)
            part = jnp.dot(
                hid[tok], jnp.concatenate([first, second], axis=1), preferred_element_type=jnp.float32
            )
            total = part if total is None else total + part
        out[...] = total.astype(out.dtype)


def grad_hidden_kernel(place, m, a0, a1, a2, a3, b0, b1, b2, b3, ahead, out, mt):
    del ahead
    x, c, h = place[1], place[2], place[4]
    own, other = (a0, a1, a2, a3), (b0, b1, b2, b3)
    for d in range(4):
        mt[256 * d : 256 * d + 256, :] = m[lax.rem(h + 4 - d, 4)]
    for k in range(4):
        tok = lax.rem(x + 4 - k, 4)
        pieces = []
        for d in range(4):
            mine, theirs = own[k][d], other[k][d]
            pieces += [jnp.where(c == 0, mine, theirs), jnp.where(c == 0, theirs, mine)]
        out[tok] = jnp.dot(
            jnp.concatenate(pieces, axis=1), mt[...], preferred_element_type=jnp.float32
        ).astype(out.dtype)


def grad_logits_kernel(g0, g1, g2, g3, w, probs, ahead, out, squares):
    del ahead
    prod = []
    for j in range(4):
        rows = pl.ds(128 * j, 128)
        total = (
            g0[rows, :]
            + g1[rows, :].astype(jnp.float32)
            + g2[rows, :].astype(jnp.float32)
            + g3[rows, :].astype(jnp.float32)
        )
        prod.append(total * w[rows, :].astype(jnp.float32))
    grads = [prod[a] + prod[b] for a, b in PAIRS]
    mean = sum(probs[k] * grads[k] for k in range(6))
    sums = jnp.zeros((128, 256), jnp.float32)
    for k in range(6):
        value = probs[k] * (grads[k] - mean) * (1.0 / TEMPER)
        out[k] = value
        sums = sums + value * value
    sums = jnp.sum(sums, axis=0, keepdims=True)
    squares[...] = jnp.broadcast_to(sums[:, :128] + sums[:, 128:], squares.shape)


def shift(value, axis, by):
    return lax.ppermute(value, axis, [(i, (i + by) % 4) for i in range(4)])


def whole(*shape):
    return pl.BlockSpec(shape, lambda i: (0,) * len(shape))


def body(hidden, upstream, down_weight, mask_logits, gumbel_noise):
    y, l, x, h, c = (lax.axis_index(a) for a in ("y", "l", "x", "h", "c"))
    place = jnp.stack([l, x, c, y, h]).astype(jnp.int32)

    with jax.named_scope("up"):
        up = [upstream] + [shift(upstream, "h", d) for d in (1, 2, 3)]
    up = pl.pallas_call(
        stack_kernel,
        out_shape=jax.ShapeDtypeStruct((4, 512, 128), jnp.bfloat16),
        grid=(1,),
        in_specs=[whole(512, 128)] * 4,
        out_specs=whole(4, 512, 128),
        cost_estimate=pl.CostEstimate(flops=10**12, bytes_accessed=1 << 30, transcendentals=0),
        name="stack_upstream",
    )(*up)

    order = np.zeros((512, 512), np.float32)
    for j in range(4):
        for g in range(128):
            order[j * 128 + g, 4 * g + j] = 1.0
    order = jnp.asarray(order, jnp.bfloat16)
    hid_t = lax.dot_general(
        order, hidden, (((1,), (1,)), ((), ())), preferred_element_type=jnp.float32
    ).astype(jnp.bfloat16)
    with jax.named_scope("hidden"):
        hid_all = lax.all_gather(hid_t, "y")

    weight = jnp.dot(order, down_weight, preferred_element_type=jnp.float32).astype(jnp.bfloat16)
    logits = jnp.transpose(mask_logits, (1, 0, 2)) + jnp.transpose(gumbel_noise, (1, 0, 2))
    probs = jax.nn.softmax(logits / TEMPER, axis=0)
    rounded = probs.astype(jnp.bfloat16).astype(jnp.float32)
    keep = [sum(rounded[k] for k in range(6) if j in PAIRS[k]) for j in range(4)]
    masked = jnp.concatenate(
        [(weight[128 * j : 128 * j + 128].astype(jnp.float32) * keep[j]).astype(jnp.bfloat16) for j in range(4)]
    )
    masked_t = lax.dot_general(
        masked, order, (((0,), (0,)), ((), ())), preferred_element_type=jnp.float32
    ).astype(jnp.bfloat16)
    with jax.named_scope("masked"):
        mt = lax.all_gather(masked_t, "l")

    with jax.named_scope("upstream_xy"):
        own = [
            lax.ppermute(up, ("y", "x"), [(b * 4 + a, a * 4 + (b + k) % 4) for b in range(4) for a in range(4)])
            for k in range(4)
        ]
    with jax.named_scope("upstream_core"):
        other = [lax.ppermute(u, "c", [(0, 1), (1, 0)]) for u in own]

    smem = pl.BlockSpec(memory_space=pltpu.SMEM)
    tall, block = whole(512, 512), whole(4, 512, 128)
    params = pltpu.CompilerParams(vmem_limit_bytes=VMEM)
    g = pl.pallas_call(
        grad_masked_kernel,
        out_shape=[jax.ShapeDtypeStruct((512, 256), jnp.float32)]
        + [jax.ShapeDtypeStruct((512, 256), jnp.bfloat16)] * 3,
        grid=(1,),
        in_specs=[smem, whole(4, 512, 512)] + [block] * 8,
        out_specs=[whole(512, 256)] * 4,
        compiler_params=params,
        cost_estimate=pl.CostEstimate(flops=2 * 512 * 2048 * 1024, bytes_accessed=7 << 20, transcendentals=0),
        name="grad_masked",
    )(place, hid_all, *own, *other)
    with jax.named_scope("grad_masked_sum"):
        got = [shift(g[e], "l", e) for e in (1, 2, 3)]

    gh = pl.pallas_call(
        grad_hidden_kernel,
        out_shape=jax.ShapeDtypeStruct((4, 512, 512), jnp.bfloat16),
        grid=(1,),
        in_specs=[smem, whole(4, 256, 512)] + [block] * 8 + [pl.BlockSpec(memory_space=pl.ANY)],
        out_specs=whole(4, 512, 512),
        scratch_shapes=[pltpu.VMEM((1024, 512), jnp.bfloat16)],
        compiler_params=params,
        cost_estimate=pl.CostEstimate(flops=2 * 512 * 2048 * 1024, bytes_accessed=7 << 20, transcendentals=0),
        name="grad_hidden",
    )(place, mt, *own, *other, g[0])
    with jax.named_scope("grad_hidden_sum"):
        grad_hidden = lax.psum_scatter(gh.reshape(2048, 512), "y", scatter_dimension=0, tiled=True)

    grad_logits, squares = pl.pallas_call(
        grad_logits_kernel,
        out_shape=[
            jax.ShapeDtypeStruct((6, 128, 256), jnp.float32),
            jax.ShapeDtypeStruct((16, 128), jnp.float32),
        ],
        grid=(1,),
        in_specs=[whole(512, 256)] * 5 + [whole(6, 128, 256), pl.BlockSpec(memory_space=pl.ANY)],
        out_specs=[whole(6, 128, 256), whole(16, 128)],
        compiler_params=params,
        cost_estimate=pl.CostEstimate(flops=10**12, bytes_accessed=1 << 30, transcendentals=0),
        name="grad_logits",
    )(g[0], *got, weight, probs, g[0])
    with jax.named_scope("mean_square"):
        squares = lax.all_to_all(squares, ("l", "h"), 0, 0, tiled=True)
        squares = jnp.broadcast_to(jnp.sum(squares, axis=0, keepdims=True), (32, 128))
        squares = lax.all_to_all(squares, ("x", "y", "c"), 0, 0, tiled=True)
    scale = lax.rsqrt(jnp.sum(squares) / (4096 * 6 * 4096) + 1e-06)
    logit_step = jnp.transpose(grad_logits * scale, (1, 0, 2))
    return grad_hidden, logit_step


def solution(mesh):
    fine = Mesh(mesh.devices.reshape(4, 4, 4, 4, 2), ("y", "l", "x", "h", "c"))
    dp, fsdp = ("y", "l"), ("x", "h", "c")
    return jax.shard_map(
        body,
        mesh=fine,
        in_specs=(
            P(dp, fsdp),
            P(dp, fsdp),
            P(fsdp, dp),
            P(fsdp, None, dp),
            P(fsdp, None, dp),
        ),
        out_specs=(P(dp, fsdp), P(fsdp, None, dp)),
        check_vma=False,
    )
```

```python
import jax
import jax.numpy as jnp
import numpy as np
from jax import lax
from jax.experimental import pallas as pl
from jax.experimental.pallas import tpu as pltpu
from jax.sharding import Mesh, PartitionSpec as P

PAIRS = ((0, 1), (0, 2), (0, 3), (1, 2), (1, 3), (2, 3))
TEMPER = 2.0
VMEM = 60 * 1024 * 1024


def stack_kernel(r0, r1, r2, r3, out):
    for d, piece in enumerate((r0, r1, r2, r3)):
        out[d] = piece[...]


def grad_masked_kernel(
    place, hid, a0, a1, a2, a3, b0, b1, b2, b3, o0, o1, o2, o3
):
    l, x, c, y, h = (place[i] for i in range(5))
    own, other = (a0, a1, a2, a3), (b0, b1, b2, b3)
    for e, out in enumerate((o0, o1, o2, o3)):
        col = lax.rem(h + 8 - l - e, 4)
        total = None
        for k in range(4):
            tok = lax.rem(x + 16 - y - k - 2 * c, 4)
            mine, theirs = own[k][col], other[(k + 2) % 4][col]
            first = jnp.where(c == 0, mine, theirs)
            second = jnp.where(c == 0, theirs, mine)
            part = jnp.dot(
                hid[tok], jnp.concatenate([first, second], axis=1), preferred_element_type=jnp.float32
            )
            total = part if total is None else total + part
        out[...] = total.astype(out.dtype)


def grad_hidden_kernel(place, m, a0, a1, a2, a3, b0, b1, b2, b3, ahead, out, mt):
    del ahead
    x, c, y, h = (place[i] for i in range(1, 5))
    own, other = (a0, a1, a2, a3), (b0, b1, b2, b3)
    for d in range(4):
        mt[256 * d : 256 * d + 256, :] = m[lax.rem(h + 4 - d, 4)]
    for k in range(4):
        tok = lax.rem(x + 16 - y - k - 2 * c, 4)
        pieces = []
        for d in range(4):
            mine, theirs = own[k][d], other[(k + 2) % 4][d]
            pieces += [jnp.where(c == 0, mine, theirs), jnp.where(c == 0, theirs, mine)]
        out[tok] = jnp.dot(
            jnp.concatenate(pieces, axis=1), mt[...], preferred_element_type=jnp.float32
        ).astype(out.dtype)


def grad_logits_kernel(g0, g1, g2, g3, w, probs, ahead, out, squares):
    del ahead
    prod = []
    for j in range(4):
        rows = pl.ds(128 * j, 128)
        total = (
            g0[rows, :]
            + g1[rows, :].astype(jnp.float32)
            + g2[rows, :].astype(jnp.float32)
            + g3[rows, :].astype(jnp.float32)
        )
        prod.append(total * w[rows, :].astype(jnp.float32))
    grads = [prod[a] + prod[b] for a, b in PAIRS]
    mean = sum(probs[k] * grads[k] for k in range(6))
    sums = jnp.zeros((128, 256), jnp.float32)
    for k in range(6):
        value = probs[k] * (grads[k] - mean) * (1.0 / TEMPER)
        out[k] = value
        sums = sums + value * value
    sums = jnp.sum(sums, axis=0, keepdims=True)
    squares[...] = jnp.broadcast_to(sums[:, :128] + sums[:, 128:], squares.shape)


def shift(value, axis, by):
    return lax.ppermute(value, axis, [(i, (i + by) % 4) for i in range(4)])


def whole(*shape):
    return pl.BlockSpec(shape, lambda i: (0,) * len(shape))


def body(hidden, upstream, down_weight, mask_logits, gumbel_noise):
    y, l, x, h, c = (lax.axis_index(a) for a in ("y", "l", "x", "h", "c"))
    place = jnp.stack([l, x, c, y, h]).astype(jnp.int32)

    with jax.named_scope("up"):
        up = [upstream] + [shift(upstream, "h", d) for d in (1, 2, 3)]
    up = pl.pallas_call(
        stack_kernel,
        out_shape=jax.ShapeDtypeStruct((4, 512, 128), jnp.bfloat16),
        grid=(1,),
        in_specs=[whole(512, 128)] * 4,
        out_specs=whole(4, 512, 128),
        cost_estimate=pl.CostEstimate(flops=10**12, bytes_accessed=1 << 30, transcendentals=0),
        name="stack_upstream",
    )(*up)

    order = np.zeros((512, 512), np.float32)
    for j in range(4):
        for g in range(128):
            order[j * 128 + g, 4 * g + j] = 1.0
    order = jnp.asarray(order, jnp.bfloat16)
    hid_t = lax.dot_general(
        order, hidden, (((1,), (1,)), ((), ())), preferred_element_type=jnp.float32
    ).astype(jnp.bfloat16)
    with jax.named_scope("hidden"):
        hid_all = lax.all_gather(hid_t, "y")

    weight = jnp.dot(order, down_weight, preferred_element_type=jnp.float32).astype(jnp.bfloat16)
    logits = jnp.transpose(mask_logits, (1, 0, 2)) + jnp.transpose(gumbel_noise, (1, 0, 2))
    probs = jax.nn.softmax(logits / TEMPER, axis=0)
    rounded = probs.astype(jnp.bfloat16).astype(jnp.float32)
    keep = [sum(rounded[k] for k in range(6) if j in PAIRS[k]) for j in range(4)]
    masked = jnp.concatenate(
        [(weight[128 * j : 128 * j + 128].astype(jnp.float32) * keep[j]).astype(jnp.bfloat16) for j in range(4)]
    )
    masked_t = lax.dot_general(
        masked, order, (((0,), (0,)), ((), ())), preferred_element_type=jnp.float32
    ).astype(jnp.bfloat16)
    with jax.named_scope("masked"):
        mt = lax.all_to_all(jnp.broadcast_to(masked_t[None], (4, 256, 512)), "l", 0, 0)

    with jax.named_scope("upstream_xy"):
        own = [
            lax.ppermute(
                up,
                ("y", "x", "c"),
                [
                    ((b * 4 + a) * 2 + core, (a * 4 + (a + b + k + 2 * core) % 4) * 2 + core)
                    for b in range(4)
                    for a in range(4)
                    for core in range(2)
                ],
            )
            for k in range(4)
        ]
    with jax.named_scope("upstream_core"):
        other = [lax.ppermute(u, "c", [(0, 1), (1, 0)]) for u in own]

    smem = pl.BlockSpec(memory_space=pltpu.SMEM)
    tall, block = whole(512, 512), whole(4, 512, 128)
    params = pltpu.CompilerParams(vmem_limit_bytes=VMEM)
    g = pl.pallas_call(
        grad_masked_kernel,
        out_shape=[jax.ShapeDtypeStruct((512, 256), jnp.float32)]
        + [jax.ShapeDtypeStruct((512, 256), jnp.bfloat16)] * 3,
        grid=(1,),
        in_specs=[smem, whole(4, 512, 512)] + [block] * 8,
        out_specs=[whole(512, 256)] * 4,
        compiler_params=params,
        cost_estimate=pl.CostEstimate(flops=2 * 512 * 2048 * 1024, bytes_accessed=7 << 20, transcendentals=0),
        name="grad_masked",
    )(place, hid_all, *own, *other)
    with jax.named_scope("grad_masked_sum"):
        got = [shift(g[e], "l", e) for e in (1, 2, 3)]

    gh = pl.pallas_call(
        grad_hidden_kernel,
        out_shape=jax.ShapeDtypeStruct((4, 512, 512), jnp.bfloat16),
        grid=(1,),
        in_specs=[smem, whole(4, 256, 512)] + [block] * 8 + [pl.BlockSpec(memory_space=pl.ANY)],
        out_specs=whole(4, 512, 512),
        scratch_shapes=[pltpu.VMEM((1024, 512), jnp.bfloat16)],
        compiler_params=params,
        cost_estimate=pl.CostEstimate(flops=2 * 512 * 2048 * 1024, bytes_accessed=7 << 20, transcendentals=0),
        name="grad_hidden",
    )(place, mt, *own, *other, g[0])
    with jax.named_scope("grad_hidden_sum"):
        grad_hidden = lax.psum_scatter(gh.reshape(2048, 512), "y", scatter_dimension=0, tiled=True)

    grad_logits, squares = pl.pallas_call(
        grad_logits_kernel,
        out_shape=[
            jax.ShapeDtypeStruct((6, 128, 256), jnp.float32),
            jax.ShapeDtypeStruct((16, 128), jnp.float32),
        ],
        grid=(1,),
        in_specs=[whole(512, 256)] * 5 + [whole(6, 128, 256), pl.BlockSpec(memory_space=pl.ANY)],
        out_specs=[whole(6, 128, 256), whole(16, 128)],
        compiler_params=params,
        cost_estimate=pl.CostEstimate(flops=10**12, bytes_accessed=1 << 30, transcendentals=0),
        name="grad_logits",
    )(g[0], *got, weight, probs, g[0])
    with jax.named_scope("mean_square"):
        squares = lax.all_to_all(squares, ("l", "h"), 0, 0, tiled=True)
        squares = jnp.broadcast_to(jnp.sum(squares, axis=0, keepdims=True), (32, 128))
        squares = lax.all_to_all(squares, ("x", "y", "c"), 0, 0, tiled=True)
    scale = lax.rsqrt(jnp.sum(squares) / (4096 * 6 * 4096) + 1e-06)
    logit_step = jnp.transpose(grad_logits * scale, (1, 0, 2))
    return grad_hidden, logit_step


def solution(mesh):
    fine = Mesh(mesh.devices.reshape(4, 4, 4, 4, 2), ("y", "l", "x", "h", "c"))
    dp, fsdp = ("y", "l"), ("x", "h", "c")
    return jax.shard_map(
        body,
        mesh=fine,
        in_specs=(
            P(dp, fsdp),
            P(dp, fsdp),
            P(fsdp, dp),
            P(fsdp, None, dp),
            P(fsdp, None, dp),
        ),
        out_specs=(P(dp, fsdp), P(fsdp, None, dp)),
        check_vma=False,
    )
```

```python
import jax
import jax.numpy as jnp
import numpy as np
from jax import lax
from jax.experimental import pallas as pl
from jax.experimental.pallas import tpu as pltpu
from jax.sharding import Mesh, PartitionSpec as P

PAIRS = ((0, 1), (0, 2), (0, 3), (1, 2), (1, 3), (2, 3))
TEMPER = 2.0
VMEM = 60 * 1024 * 1024


def stack_kernel(r0, r1, r2, r3, out):
    for d, piece in enumerate((r0, r1, r2, r3)):
        out[d] = piece[...]


def grad_masked_block(place, hid, own, other, col):
    x, c, y = place[1], place[2], place[3]
    total = None
    for k in range(4):
        tok = lax.rem(x + 16 - y - k - 2 * c, 4)
        mine, theirs = own[k][col], other[(k + 2) % 4][col]
        first = jnp.where(c == 0, mine, theirs)
        second = jnp.where(c == 0, theirs, mine)
        part = jnp.dot(
            hid[tok], jnp.concatenate([first, second], axis=1), preferred_element_type=jnp.float32
        )
        total = part if total is None else total + part
    return total


def grad_masked_far_kernel(place, hid, a0, a1, a2, a3, b0, b1, b2, b3, out):
    out[...] = grad_masked_block(place, hid, (a0, a1, a2, a3), (b0, b1, b2, b3), 0).astype(out.dtype)


def grad_masked_kernel(place, hid, a0, a1, a2, a3, b0, b1, b2, b3, far, o0, o1, o3):
    del far
    l, h = place[0], place[4]
    for e, out in ((1, o1), (3, o3), (0, o0)):
        col = lax.rem(h + 8 - l - e, 4)
        out[...] = grad_masked_block(place, hid, (a0, a1, a2, a3), (b0, b1, b2, b3), col).astype(out.dtype)


def grad_hidden_kernel(place, m, a0, a1, a2, a3, b0, b1, b2, b3, ahead, out, mt):
    del ahead
    x, c, y, h = (place[i] for i in range(1, 5))
    own, other = (a0, a1, a2, a3), (b0, b1, b2, b3)
    for d in range(4):
        mt[256 * d : 256 * d + 256, :] = m[lax.rem(h + 4 - d, 4)]
    for k in range(4):
        tok = lax.rem(x + 16 - y - k - 2 * c, 4)
        pieces = []
        for d in range(4):
            mine, theirs = own[k][d], other[(k + 2) % 4][d]
            pieces += [jnp.where(c == 0, mine, theirs), jnp.where(c == 0, theirs, mine)]
        out[tok] = jnp.dot(
            jnp.concatenate(pieces, axis=1), mt[...], preferred_element_type=jnp.float32
        ).astype(out.dtype)


def grad_logits_kernel(g0, g1, g2, g3, w, probs, ahead, out, squares):
    del ahead
    prod = []
    for j in range(4):
        rows = pl.ds(128 * j, 128)
        total = (
            g0[rows, :]
            + g1[rows, :].astype(jnp.float32)
            + g2[rows, :].astype(jnp.float32)
            + g3[rows, :].astype(jnp.float32)
        )
        prod.append(total * w[rows, :].astype(jnp.float32))
    grads = [prod[a] + prod[b] for a, b in PAIRS]
    mean = sum(probs[k] * grads[k] for k in range(6))
    sums = jnp.zeros((128, 256), jnp.float32)
    for k in range(6):
        value = probs[k] * (grads[k] - mean) * (1.0 / TEMPER)
        out[k] = value
        sums = sums + value * value
    sums = jnp.sum(sums, axis=0, keepdims=True)
    squares[...] = jnp.broadcast_to(sums[:, :128] + sums[:, 128:], squares.shape)


def shift(value, axis, by):
    return lax.ppermute(value, axis, [(i, (i + by) % 4) for i in range(4)])


def whole(*shape):
    return pl.BlockSpec(shape, lambda i: (0,) * len(shape))


def body(hidden, upstream, down_weight, mask_logits, gumbel_noise):
    y, l, x, h, c = (lax.axis_index(a) for a in ("y", "l", "x", "h", "c"))
    place = jnp.stack([l, x, c, y, h]).astype(jnp.int32)

    with jax.named_scope("up"):
        up = [upstream] + [shift(upstream, "h", d) for d in (1, 2, 3)]
    up = pl.pallas_call(
        stack_kernel,
        out_shape=jax.ShapeDtypeStruct((4, 512, 128), jnp.bfloat16),
        grid=(1,),
        in_specs=[whole(512, 128)] * 4,
        out_specs=whole(4, 512, 128),
        cost_estimate=pl.CostEstimate(flops=10**12, bytes_accessed=1 << 30, transcendentals=0),
        name="stack_upstream",
    )(*up)

    order = np.zeros((512, 512), np.float32)
    for j in range(4):
        for g in range(128):
            order[j * 128 + g, 4 * g + j] = 1.0
    order = jnp.asarray(order, jnp.bfloat16)
    hid_t = lax.dot_general(
        order, hidden, (((1,), (1,)), ((), ())), preferred_element_type=jnp.float32
    ).astype(jnp.bfloat16)
    with jax.named_scope("hidden"):
        hid_all = lax.all_gather(hid_t, "y")

    weight = jnp.dot(order, down_weight, preferred_element_type=jnp.float32).astype(jnp.bfloat16)
    logits = jnp.transpose(mask_logits, (1, 0, 2)) + jnp.transpose(gumbel_noise, (1, 0, 2))
    probs = jax.nn.softmax(logits / TEMPER, axis=0)
    rounded = probs.astype(jnp.bfloat16).astype(jnp.float32)
    keep = [sum(rounded[k] for k in range(6) if j in PAIRS[k]) for j in range(4)]
    masked = jnp.concatenate(
        [(weight[128 * j : 128 * j + 128].astype(jnp.float32) * keep[j]).astype(jnp.bfloat16) for j in range(4)]
    )
    masked_t = lax.dot_general(
        masked, order, (((0,), (0,)), ((), ())), preferred_element_type=jnp.float32
    ).astype(jnp.bfloat16)
    with jax.named_scope("masked"):
        mt = lax.all_to_all(jnp.broadcast_to(masked_t[None], (4, 256, 512)), "l", 0, 0)

    with jax.named_scope("upstream_xy"):
        own = [
            lax.ppermute(
                up,
                ("y", "x", "c"),
                [
                    ((b * 4 + a) * 2 + core, (a * 4 + (a + b + k + 2 * core) % 4) * 2 + core)
                    for b in range(4)
                    for a in range(4)
                    for core in range(2)
                ],
            )
            for k in range(4)
        ]
    with jax.named_scope("upstream_core"):
        other = [lax.ppermute(u, "c", [(0, 1), (1, 0)]) for u in own]

    smem = pl.BlockSpec(memory_space=pltpu.SMEM)
    tall, block = whole(512, 512), whole(4, 512, 128)
    params = pltpu.CompilerParams(vmem_limit_bytes=VMEM)
    piece = pl.BlockSpec((1, 512, 128), lambda i, place: (lax.rem(place[4] + 6 - place[0], 4), 0, 0))
    far = pl.pallas_call(
        grad_masked_far_kernel,
        out_shape=jax.ShapeDtypeStruct((512, 256), jnp.bfloat16),
        grid_spec=pltpu.PrefetchScalarGridSpec(
            num_scalar_prefetch=1,
            grid=(1,),
            in_specs=[pl.BlockSpec((4, 512, 512), lambda i, place: (0, 0, 0))] + [piece] * 8,
            out_specs=pl.BlockSpec((512, 256), lambda i, place: (0, 0)),
        ),
        compiler_params=params,
        cost_estimate=pl.CostEstimate(flops=2 * 512 * 512 * 1024, bytes_accessed=3 << 20, transcendentals=0),
        name="grad_masked_far",
    )(place, hid_all, *own, *other)
    near = pl.pallas_call(
        grad_masked_kernel,
        out_shape=[jax.ShapeDtypeStruct((512, 256), jnp.float32)]
        + [jax.ShapeDtypeStruct((512, 256), jnp.bfloat16)] * 2,
        grid=(1,),
        in_specs=[smem, whole(4, 512, 512)] + [block] * 8 + [pl.BlockSpec(memory_space=pl.ANY)],
        out_specs=[whole(512, 256)] * 3,
        compiler_params=params,
        cost_estimate=pl.CostEstimate(flops=2 * 512 * 1536 * 1024, bytes_accessed=6 << 20, transcendentals=0),
        name="grad_masked",
    )(place, hid_all, *own, *other, far)
    g = [near[0], near[1], far, near[2]]
    with jax.named_scope("grad_masked_sum"):
        got = [shift(g[e], "l", e) for e in (1, 2, 3)]

    gh = pl.pallas_call(
        grad_hidden_kernel,
        out_shape=jax.ShapeDtypeStruct((4, 512, 512), jnp.bfloat16),
        grid=(1,),
        in_specs=[smem, whole(4, 256, 512)] + [block] * 8 + [pl.BlockSpec(memory_space=pl.ANY)],
        out_specs=whole(4, 512, 512),
        scratch_shapes=[pltpu.VMEM((1024, 512), jnp.bfloat16)],
        compiler_params=params,
        cost_estimate=pl.CostEstimate(flops=2 * 512 * 2048 * 1024, bytes_accessed=7 << 20, transcendentals=0),
        name="grad_hidden",
    )(place, mt, *own, *other, got[1])
    with jax.named_scope("grad_hidden_sum"):
        grad_hidden = lax.psum_scatter(gh.reshape(2048, 512), "y", scatter_dimension=0, tiled=True)

    grad_logits, squares = pl.pallas_call(
        grad_logits_kernel,
        out_shape=[
            jax.ShapeDtypeStruct((6, 128, 256), jnp.float32),
            jax.ShapeDtypeStruct((16, 128), jnp.float32),
        ],
        grid=(1,),
        in_specs=[whole(512, 256)] * 5 + [whole(6, 128, 256), pl.BlockSpec(memory_space=pl.ANY)],
        out_specs=[whole(6, 128, 256), whole(16, 128)],
        compiler_params=params,
        cost_estimate=pl.CostEstimate(flops=10**12, bytes_accessed=1 << 30, transcendentals=0),
        name="grad_logits",
    )(g[0], *got, weight, probs, g[0])
    with jax.named_scope("mean_square"):
        squares = lax.all_to_all(squares, ("l", "h"), 0, 0, tiled=True)
        squares = jnp.broadcast_to(jnp.sum(squares, axis=0, keepdims=True), (32, 128))
        squares = lax.all_to_all(squares, ("x", "y", "c"), 0, 0, tiled=True)
    scale = lax.rsqrt(jnp.sum(squares) / (4096 * 6 * 4096) + 1e-06)
    logit_step = jnp.transpose(grad_logits * scale, (1, 0, 2))
    return grad_hidden, logit_step


def solution(mesh):
    fine = Mesh(mesh.devices.reshape(4, 4, 4, 4, 2), ("y", "l", "x", "h", "c"))
    dp, fsdp = ("y", "l"), ("x", "h", "c")
    return jax.shard_map(
        body,
        mesh=fine,
        in_specs=(
            P(dp, fsdp),
            P(dp, fsdp),
            P(fsdp, dp),
            P(fsdp, None, dp),
            P(fsdp, None, dp),
        ),
        out_specs=(P(dp, fsdp), P(fsdp, None, dp)),
        check_vma=False,
    )
```

```python
import jax
import jax.numpy as jnp
import numpy as np
from jax import lax
from jax.experimental import pallas as pl
from jax.experimental.pallas import tpu as pltpu
from jax.sharding import Mesh, PartitionSpec as P

PAIRS = ((0, 1), (0, 2), (0, 3), (1, 2), (1, 3), (2, 3))
TEMPER = 2.0
VMEM = 60 * 1024 * 1024


def stack_kernel(r0, r1, r2, r3, out):
    for d, piece in enumerate((r0, r1, r2, r3)):
        out[d] = piece[...]


def grad_masked_block(place, hid, own, other, col):
    x, c, y = place[1], place[2], place[3]
    total = None
    for k in range(4):
        tok = lax.rem(x + 16 - 2 * y - k - 2 * c, 4)
        mine, theirs = own[k][col], other[(k + 2) % 4][col]
        first = jnp.where(c == 0, mine, theirs)
        second = jnp.where(c == 0, theirs, mine)
        part = jnp.dot(
            hid[tok], jnp.concatenate([first, second], axis=1), preferred_element_type=jnp.float32
        )
        total = part if total is None else total + part
    return total


def grad_masked_far_kernel(place, hid, a0, a1, a2, a3, b0, b1, b2, b3, out):
    out[...] = grad_masked_block(place, hid, (a0, a1, a2, a3), (b0, b1, b2, b3), 0).astype(out.dtype)


def grad_masked_kernel(place, hid, a0, a1, a2, a3, b0, b1, b2, b3, far, o0, o1, o3):
    del far
    l, h = place[0], place[4]
    for e, out in ((1, o1), (3, o3), (0, o0)):
        col = lax.rem(h + 8 - l - e, 4)
        out[...] = grad_masked_block(place, hid, (a0, a1, a2, a3), (b0, b1, b2, b3), col).astype(out.dtype)


def grad_hidden_kernel(place, m, a0, a1, a2, a3, b0, b1, b2, b3, ahead, out, mt):
    del ahead
    x, c, y, h = (place[i] for i in range(1, 5))
    own, other = (a0, a1, a2, a3), (b0, b1, b2, b3)
    for d in range(4):
        mt[256 * d : 256 * d + 256, :] = m[lax.rem(h + 4 - d, 4)]
    for k in range(4):
        tok = lax.rem(x + 16 - 2 * y - k - 2 * c, 4)
        pieces = []
        for d in range(4):
            mine, theirs = own[k][d], other[(k + 2) % 4][d]
            pieces += [jnp.where(c == 0, mine, theirs), jnp.where(c == 0, theirs, mine)]
        out[tok] = jnp.dot(
            jnp.concatenate(pieces, axis=1), mt[...], preferred_element_type=jnp.float32
        ).astype(out.dtype)


def grad_logits_kernel(g0, g1, g3, w, probs, out, squares):
    prod = []
    for j in range(4):
        rows = pl.ds(128 * j, 128)
        total = (
            g0[rows, :]
            + g1[rows, :].astype(jnp.float32)
            + g3[rows, :].astype(jnp.float32)
        )
        prod.append(total * w[rows, :].astype(jnp.float32))
    grads = [prod[a] + prod[b] for a, b in PAIRS]
    mean = sum(probs[k] * grads[k] for k in range(6))
    sums = jnp.zeros((128, 256), jnp.float32)
    for k in range(6):
        value = probs[k] * (grads[k] - mean) * (1.0 / TEMPER)
        out[k] = value
        sums = sums + value * value
    sums = jnp.sum(sums, axis=0, keepdims=True)
    squares[...] = jnp.broadcast_to(sums[:, :128] + sums[:, 128:], squares.shape)


def shift(value, axis, by):
    return lax.ppermute(value, axis, [(i, (i + by) % 4) for i in range(4)])


def whole(*shape):
    return pl.BlockSpec(shape, lambda i: (0,) * len(shape))


def body(hidden, upstream, down_weight, mask_logits, gumbel_noise):
    y, l, x, h, c = (lax.axis_index(a) for a in ("y", "l", "x", "h", "c"))
    place = jnp.stack([l, x, c, y, h]).astype(jnp.int32)

    with jax.named_scope("up"):
        up = [upstream] + [shift(upstream, "h", d) for d in (1, 2, 3)]
    up = pl.pallas_call(
        stack_kernel,
        out_shape=jax.ShapeDtypeStruct((4, 512, 128), jnp.bfloat16),
        grid=(1,),
        in_specs=[whole(512, 128)] * 4,
        out_specs=whole(4, 512, 128),
        cost_estimate=pl.CostEstimate(flops=10**12, bytes_accessed=1 << 30, transcendentals=0),
        name="stack_upstream",
    )(*up)

    order = np.zeros((512, 512), np.float32)
    for j in range(4):
        for g in range(128):
            order[j * 128 + g, 4 * g + j] = 1.0
    order = jnp.asarray(order, jnp.bfloat16)
    hid_t = lax.dot_general(
        order, hidden, (((1,), (1,)), ((), ())), preferred_element_type=jnp.float32
    ).astype(jnp.bfloat16)
    with jax.named_scope("hidden"):
        hid_all = lax.all_gather(hid_t, "y")

    weight = jnp.dot(order, down_weight, preferred_element_type=jnp.float32).astype(jnp.bfloat16)
    logits = jnp.transpose(mask_logits, (1, 0, 2)) + jnp.transpose(gumbel_noise, (1, 0, 2))
    probs = jax.nn.softmax(logits / TEMPER, axis=0)
    rounded = probs.astype(jnp.bfloat16).astype(jnp.float32)
    keep = [sum(rounded[k] for k in range(6) if j in PAIRS[k]) for j in range(4)]
    masked = jnp.concatenate(
        [(weight[128 * j : 128 * j + 128].astype(jnp.float32) * keep[j]).astype(jnp.bfloat16) for j in range(4)]
    )
    masked_t = lax.dot_general(
        masked, order, (((0,), (0,)), ((), ())), preferred_element_type=jnp.float32
    ).astype(jnp.bfloat16)
    with jax.named_scope("masked"):
        mt = lax.all_to_all(jnp.broadcast_to(masked_t[None], (4, 256, 512)), "l", 0, 0)

    up, place = lax.optimization_barrier((up, place))
    with jax.named_scope("upstream_xy"):
        own = [
            lax.ppermute(
                up,
                ("y", "x", "c"),
                [
                    ((b * 4 + a) * 2 + core, (a * 4 + (2 * a + b + k + 2 * core) % 4) * 2 + core)
                    for b in range(4)
                    for a in range(4)
                    for core in range(2)
                ],
            )
            for k in range(4)
        ]
    with jax.named_scope("upstream_core"):
        other = [lax.ppermute(u, "c", [(0, 1), (1, 0)]) for u in own]

    smem = pl.BlockSpec(memory_space=pltpu.SMEM)
    tall, block = whole(512, 512), whole(4, 512, 128)
    params = pltpu.CompilerParams(vmem_limit_bytes=VMEM)
    piece = pl.BlockSpec((1, 512, 128), lambda i, place: (lax.rem(place[4] + 6 - place[0], 4), 0, 0))
    far = pl.pallas_call(
        grad_masked_far_kernel,
        out_shape=jax.ShapeDtypeStruct((512, 256), jnp.bfloat16),
        grid_spec=pltpu.PrefetchScalarGridSpec(
            num_scalar_prefetch=1,
            grid=(1,),
            in_specs=[pl.BlockSpec((4, 512, 512), lambda i, place: (0, 0, 0))] + [piece] * 8,
            out_specs=pl.BlockSpec((512, 256), lambda i, place: (0, 0)),
        ),
        compiler_params=params,
        cost_estimate=pl.CostEstimate(flops=2 * 512 * 512 * 1024, bytes_accessed=3 << 20, transcendentals=0),
        name="grad_masked_far",
    )(place, hid_all, *own, *other)
    near = pl.pallas_call(
        grad_masked_kernel,
        out_shape=[jax.ShapeDtypeStruct((512, 256), jnp.float32)]
        + [jax.ShapeDtypeStruct((512, 256), jnp.bfloat16)] * 2,
        grid=(1,),
        in_specs=[smem, whole(4, 512, 512)] + [block] * 8 + [pl.BlockSpec(memory_space=pl.ANY)],
        out_specs=[whole(512, 256)] * 3,
        compiler_params=params,
        cost_estimate=pl.CostEstimate(flops=2 * 512 * 1536 * 1024, bytes_accessed=6 << 20, transcendentals=0),
        name="grad_masked",
    )(place, hid_all, *own, *other, far)
    g = [near[0], near[1], far, near[2]]
    with jax.named_scope("grad_masked_sum"):
        got = [shift(g[e], "l", e) for e in (1, 2, 3)]

    gh = pl.pallas_call(
        grad_hidden_kernel,
        out_shape=jax.ShapeDtypeStruct((4, 512, 512), jnp.bfloat16),
        grid=(1,),
        in_specs=[smem, whole(4, 256, 512)] + [block] * 8 + [pl.BlockSpec(memory_space=pl.ANY)],
        out_specs=whole(4, 512, 512),
        scratch_shapes=[pltpu.VMEM((1024, 512), jnp.bfloat16)],
        compiler_params=params,
        cost_estimate=pl.CostEstimate(flops=2 * 512 * 2048 * 1024, bytes_accessed=7 << 20, transcendentals=0),
        name="grad_hidden",
    )(place, mt, *own, *other, g[0])
    with jax.named_scope("grad_hidden_sum"):
        grad_hidden = lax.psum_scatter(gh.reshape(2048, 512), "y", scatter_dimension=0, tiled=True)

    part = g[0] + got[1].astype(jnp.float32)
    grad_logits, squares = pl.pallas_call(
        grad_logits_kernel,
        out_shape=[
            jax.ShapeDtypeStruct((6, 128, 256), jnp.float32),
            jax.ShapeDtypeStruct((16, 128), jnp.float32),
        ],
        grid=(1,),
        in_specs=[whole(512, 256)] * 4 + [whole(6, 128, 256)],
        out_specs=[whole(6, 128, 256), whole(16, 128)],
        compiler_params=params,
        cost_estimate=pl.CostEstimate(flops=10**12, bytes_accessed=1 << 30, transcendentals=0),
        name="grad_logits",
    )(part, got[0], got[2], weight, probs)
    with jax.named_scope("mean_square"):
        squares = lax.all_to_all(squares, ("l", "h"), 0, 0, tiled=True)
        squares = jnp.broadcast_to(jnp.sum(squares, axis=0, keepdims=True), (32, 128))
        squares = lax.all_to_all(squares, ("x", "y", "c"), 0, 0, tiled=True)
    scale = lax.rsqrt(jnp.sum(squares) / (4096 * 6 * 4096) + 1e-06)
    logit_step = jnp.transpose(grad_logits * scale, (1, 0, 2))
    return grad_hidden, logit_step


def solution(mesh):
    fine = Mesh(mesh.devices.reshape(4, 4, 4, 4, 2), ("y", "l", "x", "h", "c"))
    dp, fsdp = ("y", "l"), ("x", "h", "c")
    return jax.shard_map(
        body,
        mesh=fine,
        in_specs=(
            P(dp, fsdp),
            P(dp, fsdp),
            P(fsdp, dp),
            P(fsdp, None, dp),
            P(fsdp, None, dp),
        ),
        out_specs=(P(dp, fsdp), P(fsdp, None, dp)),
        check_vma=False,
    )
```

```python
import jax
import jax.numpy as jnp
import numpy as np
from jax import lax
from jax.experimental import pallas as pl
from jax.experimental.pallas import tpu as pltpu
from jax.sharding import Mesh, PartitionSpec as P

PAIRS = ((0, 1), (0, 2), (0, 3), (1, 2), (1, 3), (2, 3))
TEMPER = 2.0
VMEM = 60 * 1024 * 1024


def stack_kernel(r0, r1, r2, r3, out):
    for d, piece in enumerate((r0, r1, r2, r3)):
        out[d] = piece[...]


def grad_masked_block(place, hid, own, other, col):
    x, c, y = place[1], place[2], place[3]
    total = None
    for k in range(4):
        tok = lax.rem(x + 16 - 2 * y - k - 2 * c, 4)
        mine, theirs = own[k][col], other[(k + 2) % 4][col]
        first = jnp.where(c == 0, mine, theirs)
        second = jnp.where(c == 0, theirs, mine)
        part = jnp.dot(
            hid[tok], jnp.concatenate([first, second], axis=1), preferred_element_type=jnp.float32
        )
        total = part if total is None else total + part
    return total


def grad_masked_far_kernel(place, hid, a0, a1, a2, a3, b0, b1, b2, b3, out):
    out[...] = grad_masked_block(place, hid, (a0, a1, a2, a3), (b0, b1, b2, b3), 0).astype(out.dtype)


def grad_masked_kernel(place, hid, a0, a1, a2, a3, b0, b1, b2, b3, far, o0, o1, o3):
    del far
    l, h = place[0], place[4]
    for e, out in ((1, o1), (3, o3), (0, o0)):
        col = lax.rem(h + 8 - l - e, 4)
        out[...] = grad_masked_block(place, hid, (a0, a1, a2, a3), (b0, b1, b2, b3), col).astype(out.dtype)


def grad_hidden_kernel(place, m, a0, a1, a2, a3, b0, b1, b2, b3, ahead, out, mt):
    del ahead
    x, c, y, h = (place[i] for i in range(1, 5))
    own, other = (a0, a1, a2, a3), (b0, b1, b2, b3)
    for d in range(4):
        mt[256 * d : 256 * d + 256, :] = m[lax.rem(h + 4 - d, 4)]
    for k in range(4):
        tok = lax.rem(x + 16 - 2 * y - k - 2 * c, 4)
        pieces = []
        for d in range(4):
            mine, theirs = own[k][d], other[(k + 2) % 4][d]
            pieces += [jnp.where(c == 0, mine, theirs), jnp.where(c == 0, theirs, mine)]
        out[tok] = jnp.dot(
            jnp.concatenate(pieces, axis=1), mt[...], preferred_element_type=jnp.float32
        ).astype(out.dtype)


def grad_logits_kernel(g0, g1, g3, w, probs, out, squares):
    prod = []
    for j in range(4):
        rows = pl.ds(128 * j, 128)
        total = (
            g0[rows, :]
            + g1[rows, :].astype(jnp.float32)
            + g3[rows, :].astype(jnp.float32)
        )
        prod.append(total * w[rows, :].astype(jnp.float32))
    grads = [prod[a] + prod[b] for a, b in PAIRS]
    mean = sum(probs[k] * grads[k] for k in range(6))
    sums = jnp.zeros((128, 256), jnp.float32)
    for k in range(6):
        value = probs[k] * (grads[k] - mean) * (1.0 / TEMPER)
        out[k] = value
        sums = sums + value * value
    sums = jnp.sum(sums, axis=0, keepdims=True)
    squares[...] = jnp.broadcast_to(sums[:, :128] + sums[:, 128:], squares.shape)


def shift(value, axis, by):
    return lax.ppermute(value, axis, [(i, (i + by) % 4) for i in range(4)])


def whole(*shape):
    return pl.BlockSpec(shape, lambda i: (0,) * len(shape))


def body(hidden, upstream, down_weight, mask_logits, gumbel_noise):
    y, l, x, h, c = (lax.axis_index(a) for a in ("y", "l", "x", "h", "c"))
    place = jnp.stack([l, x, c, y, h]).astype(jnp.int32)

    with jax.named_scope("up"):
        up = [upstream] + [shift(upstream, "h", d) for d in (1, 2, 3)]
    up = pl.pallas_call(
        stack_kernel,
        out_shape=jax.ShapeDtypeStruct((4, 512, 128), jnp.bfloat16),
        grid=(1,),
        in_specs=[whole(512, 128)] * 4,
        out_specs=whole(4, 512, 128),
        cost_estimate=pl.CostEstimate(flops=10**12, bytes_accessed=1 << 30, transcendentals=0),
        name="stack_upstream",
    )(*up)

    order = np.zeros((512, 512), np.float32)
    for j in range(4):
        for g in range(128):
            order[j * 128 + g, 4 * g + j] = 1.0
    order = jnp.asarray(order, jnp.bfloat16)
    hid_t = lax.dot_general(
        order, hidden, (((1,), (1,)), ((), ())), preferred_element_type=jnp.float32
    ).astype(jnp.bfloat16)
    with jax.named_scope("hidden"):
        hid_all = lax.all_gather(hid_t, "y")

    weight = jnp.dot(order, down_weight, preferred_element_type=jnp.float32).astype(jnp.bfloat16)
    logits = jnp.transpose(mask_logits, (1, 0, 2)) + jnp.transpose(gumbel_noise, (1, 0, 2))
    probs = jax.nn.softmax(logits / TEMPER, axis=0)
    rounded = probs.astype(jnp.bfloat16).astype(jnp.float32)
    keep = [sum(rounded[k] for k in range(6) if j in PAIRS[k]) for j in range(4)]
    masked = jnp.concatenate(
        [(weight[128 * j : 128 * j + 128].astype(jnp.float32) * keep[j]).astype(jnp.bfloat16) for j in range(4)]
    )
    masked_t = lax.dot_general(
        masked, order, (((0,), (0,)), ((), ())), preferred_element_type=jnp.float32
    ).astype(jnp.bfloat16)
    with jax.named_scope("masked"):
        mt = lax.all_to_all(jnp.broadcast_to(masked_t[None], (4, 256, 512)), "l", 0, 0)

    up, place = lax.optimization_barrier((up, place))
    with jax.named_scope("upstream_xy"):
        own = [
            lax.ppermute(
                up,
                ("y", "x", "c"),
                [
                    ((b * 4 + a) * 2 + core, (a * 4 + (2 * a + b + k + 2 * core) % 4) * 2 + core)
                    for b in range(4)
                    for a in range(4)
                    for core in range(2)
                ],
            )
            for k in range(4)
        ]
    with jax.named_scope("upstream_core"):
        other = [lax.ppermute(u, "c", [(0, 1), (1, 0)]) for u in own]

    smem = pl.BlockSpec(memory_space=pltpu.SMEM)
    tall, block = whole(512, 512), whole(4, 512, 128)
    params = pltpu.CompilerParams(vmem_limit_bytes=VMEM)
    piece = pl.BlockSpec((1, 512, 128), lambda i, place: (lax.rem(place[4] + 6 - place[0], 4), 0, 0))
    far = pl.pallas_call(
        grad_masked_far_kernel,
        out_shape=jax.ShapeDtypeStruct((512, 256), jnp.bfloat16),
        grid_spec=pltpu.PrefetchScalarGridSpec(
            num_scalar_prefetch=1,
            grid=(1,),
            in_specs=[pl.BlockSpec((4, 512, 512), lambda i, place: (0, 0, 0))] + [piece] * 8,
            out_specs=pl.BlockSpec((512, 256), lambda i, place: (0, 0)),
        ),
        compiler_params=params,
        cost_estimate=pl.CostEstimate(flops=2 * 512 * 512 * 1024, bytes_accessed=3 << 20, transcendentals=0),
        name="grad_masked_far",
    )(place, hid_all, *own, *other)
    near = pl.pallas_call(
        grad_masked_kernel,
        out_shape=[jax.ShapeDtypeStruct((512, 256), jnp.float32)]
        + [jax.ShapeDtypeStruct((512, 256), jnp.bfloat16)] * 2,
        grid=(1,),
        in_specs=[smem, whole(4, 512, 512)] + [block] * 8 + [pl.BlockSpec(memory_space=pl.ANY)],
        out_specs=[whole(512, 256)] * 3,
        compiler_params=params,
        cost_estimate=pl.CostEstimate(flops=2 * 512 * 1536 * 1024, bytes_accessed=6 << 20, transcendentals=0),
        name="grad_masked",
    )(place, hid_all, *own, *other, far)
    g = [near[0], near[1], far, near[2]]
    with jax.named_scope("grad_masked_sum"):
        got = [shift(g[e], "l", e) for e in (1, 2, 3)]

    gh = pl.pallas_call(
        grad_hidden_kernel,
        out_shape=jax.ShapeDtypeStruct((4, 512, 512), jnp.bfloat16),
        grid=(1,),
        in_specs=[smem, whole(4, 256, 512)] + [block] * 8 + [pl.BlockSpec(memory_space=pl.ANY)],
        out_specs=whole(4, 512, 512),
        scratch_shapes=[pltpu.VMEM((1024, 512), jnp.bfloat16)],
        compiler_params=params,
        cost_estimate=pl.CostEstimate(flops=2 * 512 * 2048 * 1024, bytes_accessed=7 << 20, transcendentals=0),
        name="grad_hidden",
    )(place, mt, *own, *other, g[0])
    with jax.named_scope("grad_hidden_sum"):
        grad_hidden = lax.psum_scatter(gh.reshape(2048, 512), "y", scatter_dimension=0, tiled=True)

    part = g[0] + got[1].astype(jnp.float32)
    grad_logits, squares = pl.pallas_call(
        grad_logits_kernel,
        out_shape=[
            jax.ShapeDtypeStruct((6, 128, 256), jnp.float32),
            jax.ShapeDtypeStruct((16, 128), jnp.float32),
        ],
        in_specs=[pl.BlockSpec(memory_space=pltpu.VMEM)] * 5,
        out_specs=[pl.BlockSpec(memory_space=pltpu.VMEM)] * 2,
        compiler_params=pltpu.CompilerParams(vmem_limit_bytes=16 << 20),
        cost_estimate=pl.CostEstimate(flops=10**12, bytes_accessed=1 << 30, transcendentals=0),
        name="grad_logits",
    )(part, got[0], got[2], weight, probs)
    with jax.named_scope("mean_square"):
        squares = lax.all_to_all(squares, ("l", "h"), 0, 0, tiled=True)
        squares = jnp.broadcast_to(jnp.sum(squares, axis=0, keepdims=True), (32, 128))
        squares = lax.all_to_all(squares, ("x", "y", "c"), 0, 0, tiled=True)
    scale = lax.rsqrt(jnp.sum(squares) / (4096 * 6 * 4096) + 1e-06)
    logit_step = jnp.transpose(grad_logits * scale, (1, 0, 2))
    return grad_hidden, logit_step


def solution(mesh):
    fine = Mesh(mesh.devices.reshape(4, 4, 4, 4, 2), ("y", "l", "x", "h", "c"))
    dp, fsdp = ("y", "l"), ("x", "h", "c")
    return jax.shard_map(
        body,
        mesh=fine,
        in_specs=(
            P(dp, fsdp),
            P(dp, fsdp),
            P(fsdp, dp),
            P(fsdp, None, dp),
            P(fsdp, None, dp),
        ),
        out_specs=(P(dp, fsdp), P(fsdp, None, dp)),
        check_vma=False,
    )
```
